32 devices in a mesh: dp: 4 (over x, core), seq: 8 (over z, y).
Axes of the slice: x: 2, y: 2, z: 4, core: 2. Of those that a mesh axis runs over, the one named last changes fastest.
Arguments:
- glu_out: bfloat16 [4, 1024, 1536], P('dp', 'seq'), may hold values from -6 to 6
- lengths: int32 [4], replicated, may hold values from 128 to 1024, as said below
- kernel: float32 [31, 1536], replicated, may hold values from -1 to 1
- gain: float32 [1536], replicated, may hold values from 0.25 to 1.75
- bias: float32 [1536], replicated, may hold values from -3 to 3
- weight: bfloat16 [1536, 1536], P(('dp', 'seq')), may hold values from -0.15625 to 0.15625
- master: float32 [1536, 1536], P(('dp', 'seq')), may hold values from -0.15625 to 0.15625
- moment_one: float32 [1536, 1536], P(('dp', 'seq')), may hold values from -120 to 120
- moment_two: float32 [1536, 1536], P(('dp', 'seq')), may hold values from 100 to 100000
- cotangent: bfloat16 [4, 1024, 1536], P('dp', 'seq'), may hold values from -6 to 6
Outputs:
- module_out: bfloat16 [4, 1024, 1536], P('dp', 'seq')
- input_grad: bfloat16 [4, 1024, 1536], P('dp', 'seq')
- kernel_grad: float32 [31, 1536], replicated
- gain_grad: float32 [1536], replicated
- bias_grad: float32 [1536], replicated
- new_master: float32 [1536, 1536], P(('dp', 'seq'))
- new_one: float32 [1536, 1536], P(('dp', 'seq'))
- new_two: float32 [1536, 1536], P(('dp', 'seq'))
The draws below stay inside these ranges and needn't reach their ends.
Inputs may be any that keep to these rules, and one draw needn't show every extreme that they name: `lengths`: in every draw one stream has all 1024 frames valid; each other stream has between 128 and 341 valid frames.
All inputs are finite; a program needn't handle non-finite values.
Results may differ from the reference program's by a relative error of at most 0.0049.
Values may be sent and summed in bfloat16 or wider, within the bound.
A program may use at most 64 MiB of HBM per device.

```python
import math
import jax
import jax.numpy as jnp
from jax import lax

D = 1536
KERNEL = 31
HALF = 15
LENGTH = 1024
STREAMS = 4


def draw_lengths(key, part):
    first_key = jax.random.fold_in(key, 11)
    second_key = jax.random.fold_in(key, 23)
    shorter = jax.random.randint(first_key, (STREAMS,), LENGTH // 8, LENGTH // 3 + 1)
    longest = jax.random.randint(second_key, (), 0, STREAMS)
    return jnp.where(jnp.arange(STREAMS) == longest, LENGTH, shorter).astype(jnp.int32)


def block_scale(own_key, extent, cuts, smallest, high):
    level, own = 1.0, jax.random.fold_in(own_key, 6)
    for position, shards_of in cuts:
        draws = jnp.exp(jax.random.uniform(jax.random.fold_in(own, position), (shards_of,), jnp.float32, smallest / len(cuts), high / len(cuts)))
        level = level * jnp.repeat(draws, extent[position] // shards_of).reshape([-1 if axis == position else 1 for axis in range(len(extent))])
    return level


def bell_draw(own_key, shape, scale, reach, shards=(), held_as=jnp.bfloat16):
    result = scale * jax.random.normal(own_key, shape, jnp.float32)
    if shards:
        result = result * block_scale(own_key, shape, shards, -0.22, 0.18)
    return jnp.clip(result, -reach, reach).astype(held_as)


def setup_inputs(seed: int = 0) -> dict:
    key_list = jax.random.split(jax.random.key(seed), 11)
    glu_out = bell_draw(key_list[0], (STREAMS, LENGTH, D), 1.0, 6.0, ((0, 4), (1, 8)))
    lengths = draw_lengths(jax.random.fold_in(key_list[10], 71), 0)
    kernel = bell_draw(key_list[2], (KERNEL, D), KERNEL ** -0.5, 1.0, (), jnp.float32)
    gain = jnp.clip(1.0 + 0.15 * jax.random.normal(key_list[3], (D,), jnp.float32), 0.25, 1.75)
    bias = bell_draw(key_list[4], (D,), 0.5, 3.0, (), jnp.float32)
    weight = bell_draw(key_list[5], (D, D), D ** -0.5, 0.15625, ((0, 32),))
    master = bell_draw(key_list[6], (D, D), D ** -0.5, 0.15625, ((0, 32),), jnp.float32)
    moment_one = bell_draw(key_list[7], (D, D), 20.0, 120.0, ((0, 32),), jnp.float32)
    moment_two = jnp.clip(jnp.exp(math.log(100000.0) - 6.9077553 * jax.random.uniform(key_list[8], (D, D), jnp.float32) ** block_scale(key_list[8], (D, D), ((0, 32),), -0.2, 0.2)), 100.0, 100000.0)
    cotangent = bell_draw(key_list[9], (STREAMS, LENGTH, D), 1.0, 6.0, ((0, 4), (1, 8)))
    return {"glu_out": glu_out, "lengths": lengths, "kernel": kernel, "gain": gain, "bias": bias, "weight": weight, "master": master, "moment_one": moment_one, "moment_two": moment_two, "cotangent": cotangent}


beta_one = 0.9
beta_two = 0.999
adam_rate = 0.001
adam_eps = 1e-08
norm_eps = 1e-05
first_fix = 0.9999734386011124
second_fix = 0.09520785288629043

def taps_apply(padded, kernel, width):
    total = jnp.zeros((width, padded.shape[1]), jnp.float32)
    for tap in range(KERNEL):
        total = total + kernel[tap] * padded[tap:tap + width]
    return total

def prepare(glu_out, lengths, kernel, stream):
    positions = jnp.arange(LENGTH, dtype=jnp.int32)
    valid = (positions < lengths[stream])[:, None]
    masked = jnp.where(valid, glu_out[stream], jnp.zeros((), glu_out.dtype))
    padded = jnp.pad(masked.astype(jnp.float32), ((HALF, HALF), (0, 0)))
    conv_out = taps_apply(padded, kernel, LENGTH)
    return (valid, padded, conv_out)

def backward_part(glu_out, lengths, kernel, gain, bias, weight, cotangent, stream, channel_mean, inv_std):
    valid, padded, conv_out = prepare(glu_out, lengths, kernel, stream)
    standard = (conv_out - channel_mean) * inv_std
    scaled = gain * standard + bias
    logistic = jax.nn.sigmoid(scaled)
    hidden = (scaled * logistic).astype(jnp.bfloat16)
    grad_out = jnp.where(valid, cotangent[stream], jnp.zeros((), cotangent.dtype))
    hidden_grad = lax.dot_general(grad_out, weight, (((1,), (1,)), ((), ())), preferred_element_type=jnp.float32)
    scaled_grad = hidden_grad * logistic * (1.0 + scaled * (1.0 - logistic))
    return (valid, padded, standard, hidden, grad_out, scaled_grad)

def reference(glu_out, lengths, kernel, gain, bias, weight, master, moment_one, moment_two, cotangent):
    count = jnp.sum(lengths).astype(jnp.float32)
    total = jnp.zeros((D,), jnp.float32)
    for stream in range(STREAMS):
        valid, padded, conv_out = prepare(glu_out, lengths, kernel, stream)
        total = total + lax.optimization_barrier(jnp.sum(jnp.where(valid, conv_out, 0.0), axis=0))
    channel_mean = total / count
    spread = jnp.zeros((D,), jnp.float32)
    for stream in range(STREAMS):
        valid, padded, conv_out = prepare(glu_out, lengths, kernel, stream)
        spread = spread + lax.optimization_barrier(jnp.sum(jnp.where(valid, (conv_out - channel_mean) ** 2, 0.0), axis=0))
    inv_std = lax.rsqrt(spread / count + norm_eps)
    outputs = []
    weight_grad = jnp.zeros((D, D), jnp.float32)
    gain_grad = jnp.zeros((D,), jnp.float32)
    bias_grad = jnp.zeros((D,), jnp.float32)
    for stream in range(STREAMS):
        valid, padded, standard, hidden, grad_out, scaled_grad = backward_part(glu_out, lengths, kernel, gain, bias, weight, cotangent, stream, channel_mean, inv_std)
        product = jnp.dot(hidden, weight, preferred_element_type=jnp.float32)
        outputs.append(jnp.where(valid, product, 0.0).astype(jnp.bfloat16))
        weight_grad = weight_grad + lax.dot_general(hidden, grad_out, (((0,), (0,)), ((), ())), preferred_element_type=jnp.float32)
        gain_grad = gain_grad + lax.optimization_barrier(jnp.sum(scaled_grad * standard, axis=0))
        bias_grad = bias_grad + lax.optimization_barrier(jnp.sum(scaled_grad, axis=0))
    grads_in = []
    kernel_grad = jnp.zeros((KERNEL, D), jnp.float32)
    for stream in range(STREAMS):
        valid, padded, standard, hidden, grad_out, scaled_grad = backward_part(glu_out, lengths, kernel, gain, bias, weight, cotangent, stream, channel_mean, inv_std)
        conv_grad = jnp.where(valid, inv_std * (gain * scaled_grad - gain * bias_grad / count - standard * gain * gain_grad / count), 0.0)
        rows_grad = []
        for tap in range(KERNEL):
            rows_grad.append(lax.optimization_barrier(jnp.sum(conv_grad * padded[tap:tap + LENGTH], axis=0)))
        kernel_grad = kernel_grad + jnp.stack(rows_grad)
        grad_pad = jnp.pad(conv_grad, ((HALF, HALF), (0, 0)))
        flipped = jnp.zeros((LENGTH, D), jnp.float32)
        for tap in range(KERNEL):
            flipped = flipped + kernel[tap] * grad_pad[2 * HALF - tap:2 * HALF - tap + LENGTH]
        grads_in.append(jnp.where(valid, flipped, 0.0).astype(jnp.bfloat16))
    new_one = beta_one * moment_one + (1.0 - beta_one) * weight_grad
    new_two = beta_two * moment_two + (1.0 - beta_two) * weight_grad * weight_grad
    new_master = master - adam_rate * (new_one / first_fix) / (jnp.sqrt(new_two / second_fix) + adam_eps)
    return (jnp.stack(outputs), jnp.stack(grads_in), kernel_grad, gain_grad, bias_grad, new_master, new_one, new_two)
```

```python
import functools

import jax
import jax.numpy as jnp
from jax import lax
from jax.experimental import pallas as pl
from jax.experimental.pallas import tpu as pltpu
from jax.sharding import PartitionSpec as P

KERNEL = 31
HALF = 15


beta_one = 0.9
beta_two = 0.999
adam_rate = 0.001
adam_eps = 1e-08
norm_eps = 1e-05
first_fix = 0.9999734386011124
second_fix = 0.09520785288629043


def with_halo(block, sides, width):
    for axis, dim in sides:
        count = lax.axis_size(axis)
        forward = [(i, i + 1) for i in range(count - 1)]
        backward = [(target, source) for source, target in forward]
        low = lax.ppermute(
            lax.slice_in_dim(block, block.shape[dim] - width, None, axis=dim), axis, forward
        )
        high = lax.ppermute(lax.slice_in_dim(block, 0, width, axis=dim), axis, backward)
        block = jnp.concatenate([low, block, high], axis=dim)
    return block


MESH = pl.DeviceIdType.MESH
LANES = 128
AXES = ("dp", "seq")


def greet(sizes):
    barrier = pltpu.get_barrier_semaphore()
    for axis in AXES:
        me = lax.axis_index(axis)
        for step in range(1, sizes[axis]):
            pl.semaphore_signal(
                barrier,
                inc=1,
                device_id={axis: lax.rem(me + step, sizes[axis])},
                device_id_type=MESH,
            )
    pl.semaphore_wait(barrier, sizes["dp"] + sizes["seq"] - 2)


def exchange(axis, size, source, target, send_sem, recv_sem):
    me = lax.axis_index(axis)
    copies = []
    for step in range(1, size):
        peer = lax.rem(me + step, size)
        copy = pltpu.make_async_remote_copy(
            src_ref=source(peer),
            dst_ref=target(me),
            send_sem=send_sem.at[step],
            recv_sem=recv_sem.at[step],
            device_id={axis: peer},
            device_id_type=MESH,
        )
        copy.start()
        copies.append(copy)
    return copies


def finish(copies):
    for copy in copies:
        copy.wait()


def plain_sum(slots, count):
    total = slots[0]
    for i in range(1, count):
        total = total + slots[i]
    return total


def moments(slots, frames, count):
    half = slots.shape[1] // 2
    sums = [slots[i][:half] for i in range(count)]
    have = [frames[i] for i in range(count)]
    total, spread, members = sums[0], slots[0][half:], have[0]
    for i in range(1, count):
        total, spread, members = total + sums[i], spread + slots[i][half:], members + have[i]
    mean = total / jnp.maximum(members, 1.0)
    for i in range(count):
        off = sums[i] / jnp.maximum(have[i], 1.0) - mean
        spread = spread + have[i] * off * off
    return total, spread


def small_kernel(sizes, joined, x_ref, *rest):
    if joined:
        dp_frames, seq_frames, *rest = rest
    out_ref, first, second, send_a, recv_a, send_b, recv_b = rest
    stream, shard = lax.axis_index("dp"), lax.axis_index("seq")
    half = x_ref.shape[0] // 2
    greet(sizes)
    copies = exchange(
        "dp", sizes["dp"], lambda p: x_ref, lambda m: first.at[m], send_a, recv_a
    )
    first[stream] = x_ref[...]
    finish(copies)
    if joined:
        total, spread = moments(first, dp_frames, sizes["dp"])
        second[shard, :half] = total
        second[shard, half:] = spread
    else:
        second[shard] = plain_sum(first, sizes["dp"])
    copies = exchange(
        "seq",
        sizes["seq"],
        lambda p: second.at[shard],
        lambda m: second.at[m],
        send_b,
        recv_b,
    )
    finish(copies)
    if joined:
        total, spread = moments(second, seq_frames, sizes["seq"])
        out_ref[:half] = total
        out_ref[half:] = spread
    else:
        out_ref[...] = plain_sum(second, sizes["seq"])


def sems(sizes, axis):
    return [pltpu.SemaphoreType.DMA((sizes[axis],))] * 2


def small_reduce(rows, ident, frames=None):
    sizes = {axis: lax.axis_size(axis) for axis in AXES}
    flat = rows.reshape(-1, LANES)
    args = [flat] if frames is None else [flat, *frames]
    out = pl.pallas_call(
        functools.partial(small_kernel, sizes, frames is not None),
        out_shape=jax.ShapeDtypeStruct(flat.shape, jnp.float32),
        in_specs=[pl.BlockSpec(memory_space=pltpu.VMEM)] * len(args),
        out_specs=pl.BlockSpec(memory_space=pltpu.VMEM),
        scratch_shapes=[
            pltpu.VMEM((sizes["dp"], *flat.shape), jnp.float32),
            pltpu.VMEM((sizes["seq"], *flat.shape), jnp.float32),
            *sems(sizes, "dp"),
            *sems(sizes, "seq"),
        ],
        compiler_params=pltpu.CompilerParams(collective_id=ident, has_side_effects=True),
    )(*args)
    return out.reshape(rows.shape)


def wide_kernel(sizes, x_ref, out_ref, first, second, *sem):
    stream, shard = lax.axis_index("dp"), lax.axis_index("seq")
    greet(sizes)
    copies = exchange(
        "dp", sizes["dp"], lambda p: x_ref.at[p], lambda m: first.at[m], sem[0], sem[1]
    )
    first[stream] = x_ref[stream]
    finish(copies)
    first[stream] = plain_sum(first, sizes["dp"])
    copies = exchange(
        "seq",
        sizes["seq"],
        lambda p: first.at[stream, p],
        lambda m: second.at[m],
        sem[2],
        sem[3],
    )
    second[shard] = first[stream, shard]
    finish(copies)
    out_ref[stream, shard] = plain_sum(second, sizes["seq"])
    finish(
        exchange(
            "seq",
            sizes["seq"],
            lambda p: out_ref.at[stream, shard],
            lambda m: out_ref.at[stream, m],
            sem[4],
            sem[5],
        )
    )
    finish(
        exchange(
            "dp",
            sizes["dp"],
            lambda p: out_ref.at[stream],
            lambda m: out_ref.at[m],
            sem[6],
            sem[7],
        )
    )


def wide_reduce(rows, ident):
    sizes = {axis: lax.axis_size(axis) for axis in AXES}
    shares = sizes["dp"] * sizes["seq"]
    flat = rows.reshape(-1, LANES)
    unit = -(-flat.shape[0] // (shares * 8)) * 8
    padded = jnp.pad(flat, ((0, shares * unit - flat.shape[0]), (0, 0)))
    blocks = padded.reshape(sizes["dp"], sizes["seq"], unit, LANES)
    out = pl.pallas_call(
        functools.partial(wide_kernel, sizes),
        out_shape=jax.ShapeDtypeStruct(blocks.shape, jnp.float32),
        in_specs=[pl.BlockSpec(memory_space=pltpu.VMEM)],
        out_specs=pl.BlockSpec(memory_space=pltpu.VMEM),
        scratch_shapes=[
            pltpu.VMEM(blocks.shape, jnp.float32),
            pltpu.VMEM(blocks.shape[1:], jnp.float32),
            *sems(sizes, "dp"),
            *sems(sizes, "seq"),
            *sems(sizes, "seq"),
            *sems(sizes, "dp"),
        ],
        compiler_params=pltpu.CompilerParams(collective_id=ident, has_side_effects=True),
    )(blocks)
    return out.reshape(-1, LANES)[: flat.shape[0]].reshape(rows.shape)


def on_device(
    glu_out, lengths, kernel, gain, bias, weight, master, moment_one, moment_two, cotangent
):
    frames = glu_out.shape[1]
    stream = lax.axis_index("dp")
    shard = lax.axis_index("seq")
    positions = shard * frames + jnp.arange(frames, dtype=jnp.int32)
    valid = (positions < lengths[stream])[:, None]
    count = jnp.sum(lengths).astype(jnp.float32)
    masked = jnp.where(valid, glu_out[0], jnp.zeros((), glu_out.dtype))
    padded = with_halo(masked, (("seq", 0),), HALF).astype(jnp.float32)
    conv_out = jnp.zeros((frames, masked.shape[1]), jnp.float32)
    for tap in range(KERNEL):
        conv_out = conv_out + kernel[tap] * padded[tap : tap + frames]
    shards = lax.axis_size("seq")
    held = jnp.clip(lengths[:, None] - frames * jnp.arange(shards)[None], 0, frames)
    held = held.astype(jnp.float32)
    own = held[stream, shard]
    dp_frames = jnp.broadcast_to(held[:, shard][:, None, None], (held.shape[0], 1, LANES))
    seq_frames = jnp.broadcast_to(jnp.sum(held, axis=0)[:, None, None], (shards, 1, LANES))
    own_sum = jnp.sum(jnp.where(valid, conv_out, 0.0), axis=0)
    own_off = jnp.where(valid, conv_out - own_sum / jnp.maximum(own, 1.0), 0.0)
    own_spread = jnp.sum(own_off * own_off, axis=0)
    total, spread = small_reduce(
        jnp.stack([own_sum, own_spread]), 0, (dp_frames, seq_frames)
    )
    channel_mean = total / count
    channel_var = spread / count
    inv_std = lax.rsqrt(channel_var + norm_eps)
    standard = (conv_out - channel_mean) * inv_std
    scaled = gain * standard + bias
    logistic = jax.nn.sigmoid(scaled)
    hidden = (scaled * logistic).astype(jnp.bfloat16)
    grad_out = jnp.where(valid, cotangent[0], jnp.zeros((), cotangent.dtype))
    columns = hidden
    product = jnp.dot(
        columns,
        lax.all_gather(weight, ("dp", "seq"), axis=0, tiled=True),
        preferred_element_type=jnp.float32,
    )
    hidden_grad = lax.dot_general(
        grad_out,
        lax.all_gather(weight, ("dp", "seq"), axis=0, tiled=True),
        (((1,), (1,)), ((), ())),
        preferred_element_type=jnp.float32,
    )
    module_out = jnp.where(valid, product, 0.0).astype(jnp.bfloat16)
    scaled_grad = hidden_grad * logistic * (1.0 + scaled * (1.0 - logistic))
    gain_grad, bias_grad = small_reduce(
        jnp.stack([jnp.sum(scaled_grad * standard, axis=0), jnp.sum(scaled_grad, axis=0)]), 1
    )
    conv_grad = jnp.where(
        valid,
        inv_std
        * (gain * scaled_grad - gain * bias_grad / count - standard * gain * gain_grad / count),
        0.0,
    )
    grad_pad = with_halo(conv_grad, (("seq", 0),), HALF)
    flipped = jnp.zeros((frames, conv_grad.shape[1]), jnp.float32)
    for tap in range(KERNEL):
        flipped = flipped + kernel[tap] * grad_pad[2 * HALF - tap : 2 * HALF - tap + frames]
    input_grad = jnp.where(valid, flipped, 0.0).astype(jnp.bfloat16)
    tap_rows = []
    for tap in range(KERNEL):
        tap_rows.append(jnp.sum(conv_grad * padded[tap : tap + frames], axis=0))
    kernel_grad = wide_reduce(jnp.stack(tap_rows), 2)
    columns = hidden
    weight_grad = lax.psum_scatter(
        lax.dot_general(
            columns, grad_out, (((0,), (0,)), ((), ())), preferred_element_type=jnp.float32
        ).astype(jnp.bfloat16),
        ("dp", "seq"),
        scatter_dimension=0,
        tiled=True,
    ).astype(jnp.float32)
    new_one = beta_one * moment_one + (1.0 - beta_one) * weight_grad
    new_two = beta_two * moment_two + (1.0 - beta_two) * weight_grad * weight_grad
    new_master = master - adam_rate * (new_one / first_fix) / (
        jnp.sqrt(new_two / second_fix) + adam_eps
    )
    return (
        module_out[None],
        input_grad[None],
        kernel_grad,
        gain_grad,
        bias_grad,
        new_master,
        new_one,
        new_two,
    )


def solution(mesh):
    return jax.shard_map(
        on_device,
        mesh=mesh,
        in_specs=(
            P("dp", "seq", None),
            P(),
            P(),
            P(),
            P(),
            P(("dp", "seq"), None),
            P(("dp", "seq"), None),
            P(("dp", "seq"), None),
            P(("dp", "seq"), None),
            P("dp", "seq", None),
        ),
        out_specs=(
            P("dp", "seq", None),
            P("dp", "seq", None),
            P(),
            P(),
            P(),
            P(("dp", "seq"), None),
            P(("dp", "seq"), None),
            P(("dp", "seq"), None),
        ),
        check_vma=False,
    )
```
